32 devices in a mesh: grp: 4 (over z), dev: 8 (over y, x, core).
Axes of the slice: x: 2, y: 2, z: 4, core: 2. Of those that a mesh axis runs over, the one named last changes fastest.
Arguments:
- ssm_input: bfloat16 [1024, 4096], P('grp', 'dev'), may hold values from -6 to 6
- gate_input: bfloat16 [1024, 4096], P('grp', 'dev'), may hold values from -6 to 6
- step_size: float32 [1024, 64], P('grp', 'dev'), may hold values from 0.00024414062 to 0.3375
- decay_rate: float32 [64], P('dev'), may hold values from 0.5 to 2
- in_coeff: bfloat16 [1024, 128], P('grp'), may hold values from -6 to 6
- out_coeff: bfloat16 [1024, 128], P('grp'), may hold values from -6 to 6
- skip_gain: float32 [64], P('dev'), may hold values from 0.5 to 3
- norm_gain: float32 [4096], P('dev'), may hold values from 0.5 to 1.5
- out_proj: bfloat16 [4096, 2048], P(None, 'dev'), may hold values from -0.09375 to 0.09375
- residual: bfloat16 [1024, 2048], P(('grp', 'dev')), may hold values from -6 to 6
- ffn_gain: float32 [2048], replicated, may hold values from 0.5 to 1.5
- router: float32 [2048, 4], replicated, may hold values from -0.125 to 0.125
- routes: int32 [1024, 2], P(('grp', 'dev')), may hold values from 0 to 3, all different within a row; in each aligned block of 32 rows (0 to 31, 32 to 63, ...) at most 32 rows name the same one
- gate_weight: bfloat16 [4, 2048, 8192], P('grp', None, 'dev'), may hold values from -0.125 to 0.125
- up_weight: bfloat16 [4, 2048, 8192], P('grp', None, 'dev'), may hold values from -0.125 to 0.125
- down_weight: bfloat16 [4, 8192, 2048], P('grp', 'dev'), may hold values from -0.0625 to 0.0625
Outputs:
- moe_out: bfloat16 [1024, 2048], P(('grp', 'dev'))
The draws below stay inside these ranges and needn't reach their ends.
Inputs may be any that keep to these rules, and one draw needn't show every extreme that they name: `routes`: each row names two different experts; among the 32 rows of one dispatch block of consecutive tokens no expert is named more than 32 times, a bound that some block reaches.
All inputs are finite; a program needn't handle non-finite values.
Results may differ from the reference program's by a relative error of at most 0.012.
Values may be sent and summed in bfloat16 or wider, within the bound.
A program may use at most 64 MiB of HBM per device.

```python
import math
import jax
import jax.numpy as jnp
import numpy as np
from jax import lax

MODEL_DIM = 2048
NUM_HEADS = 64
HEAD_DIM = 64
STATE_DIM = 128
HIDDEN_DIM = 8192
EXPERTS = 4
STRING_LENGTH = 1024
TOK_DEV = 32
INNER_DIM = 4096
HID_DEV = 1024
SLOT_CAP = 32


def draw_step_size(key, part):
    gradual_seed, jagged_seed, spike_seed = jax.random.split(key, 3)
    slow_share = 0.5
    slow_heads = jax.random.bernoulli(gradual_seed, slow_share, (NUM_HEADS,))
    jaggedness = jax.random.uniform(jagged_seed, (STRING_LENGTH, NUM_HEADS), jnp.float32, 0.5, 1.5)
    baseline_frequency = jnp.where(slow_heads, 0.5 / STRING_LENGTH, 1.0 / 40.0)
    spike_indices = jax.random.randint(spike_seed, (4,), 0, STRING_LENGTH)
    element_ordinals = jnp.arange(STRING_LENGTH)
    spike_present = jnp.any(element_ordinals[:, None] == spike_indices[None, :], axis=1)
    return (baseline_frequency[None, :] * jaggedness + jnp.where(spike_present, 0.3, 0.0)[:, None]).astype(jnp.float32)


def block_levels(own_key, dims, cuts, least, top_value):
    factor_of, own = 1.0, jax.random.fold_in(own_key, 6)
    for position, shards_of in cuts:
        draws = jnp.exp(jax.random.uniform(jax.random.fold_in(own, position), (shards_of,), jnp.float32, least / len(cuts), top_value / len(cuts)))
        factor_of = factor_of * jnp.repeat(draws, dims[position] // shards_of).reshape([-1 if axis == position else 1 for axis in range(len(dims))])
    return factor_of


def routed_block(rng, own, number, rows, amount, top, reach, slope):
    order = jax.random.permutation(rng, amount)
    heavy_load, common = shares(amount, rows * top, reach, slope, True), shares(amount, rows * top, reach, slope, False)
    places = jnp.arange(amount)

    def named(sizes, offset_by):
        used = int((sizes > 0).sum())
        fixed = max(1, used // 4)
        shifted = fixed + (places - fixed + offset_by * (used - fixed)) % max(1, amount - fixed)
        return jnp.zeros((amount,), jnp.int32).at[order[jnp.where(places < fixed, places, shifted)]].set(jnp.asarray(sizes, jnp.int32))

    sizes = jnp.where(number % 4 == 0, named(heavy_load, number // 4), named(common, number - number // 4 - 1))
    mixed = jax.random.permutation(jax.random.fold_in(own, 3), amount)
    donor, sink = mixed[0:amount // 2 * 2:2], mixed[1:amount // 2 * 2:2]
    slack = jnp.minimum(sizes[donor] - 1, reach - sizes[sink]) // 2
    slack = jnp.where((donor == order[0]) | (sink == order[0]) | (sizes[sink] == 0), 0, jnp.maximum(slack, 0))
    shifted = jax.random.randint(jax.random.fold_in(own, 4), (amount // 2,), 0, 1 << 20) % (slack + 1)
    sizes = sizes.at[donor].add(-shifted).at[sink].add(shifted)
    items = jnp.searchsorted(jnp.cumsum(sizes), jnp.arange(rows * top), side="right").astype(jnp.int32)
    table = items.reshape(top, rows).T
    table = table[jax.random.permutation(jax.random.fold_in(own, 1), rows)]
    offset_by = jax.random.randint(jax.random.fold_in(own, 2), (rows, 1), 0, top)
    return jnp.take_along_axis(table, (jnp.arange(top)[None, :] + offset_by) % top, axis=1)


def shares(amount, total, limit, slope, full):
    loads = [(1 << 20) // math.isqrt(standing ** slope) + 1 for standing in range(1, amount + 1)]
    largest = limit if full else min(limit, max(-(-total // amount), total * loads[0] // sum(loads)))
    least = 1 if total - largest >= amount - 1 else 0
    holding, spare = [largest] + [least] * (amount - 1), total - largest - least * (amount - 1)
    while spare > 0:
        candidates = [i for i in range(1, amount) if holding[i] < largest] or [i for i in range(1, amount) if holding[i] < limit]
        mass, remaining = sum([loads[i] for i in candidates]), spare
        for i in candidates:
            more = min(limit - holding[i], max(1, remaining * loads[i] // mass), spare)
            holding[i] = holding[i] + more
            spare = spare - more
    return np.array(holding)


def centred(rng, shape, width, limit, shards=(), kind=jnp.bfloat16):
    result = jax.random.normal(rng, shape, jnp.float32) * width
    if len(shards) > 0:
        result = block_levels(rng, shape, shards, -0.22, 0.18) * result
    return jnp.clip(result, min=-limit, max=limit).astype(kind)


def setup_inputs(seed: int = 0) -> dict:
    key_of = jax.random.split(jax.random.key(seed), 17)
    ssm_input = centred(key_of[0], (STRING_LENGTH, INNER_DIM), 1.0, 6.0, ((0, 4), (1, 8)))
    gate_input = centred(key_of[1], (STRING_LENGTH, INNER_DIM), 1.0, 6.0, ((0, 4), (1, 8)))
    step_size = draw_step_size(jax.random.fold_in(key_of[16], 71), 0)
    decay_rate = jnp.clip(jnp.exp(math.log(2.0) - 1.3862944 * jax.random.uniform(key_of[3], (NUM_HEADS,), jnp.float32) ** block_levels(key_of[3], (NUM_HEADS,), ((0, 8),), -0.2, 0.2)), 0.5, 2.0)
    in_coeff = centred(key_of[4], (STRING_LENGTH, STATE_DIM), 1.0, 6.0, ((0, 4),))
    out_coeff = centred(key_of[5], (STRING_LENGTH, STATE_DIM), 1.0, 6.0, ((0, 4),))
    skip_gain = jnp.clip(jnp.exp(math.log(3.0) - 1.7917595 * jax.random.uniform(key_of[6], (NUM_HEADS,), jnp.float32) ** block_levels(key_of[6], (NUM_HEADS,), ((0, 8),), -0.2, 0.2)), 0.5, 3.0)
    norm_gain = jnp.clip(1.0 + 0.1 * jax.random.normal(key_of[7], (INNER_DIM,), jnp.float32), 0.5, 1.5)
    out_proj = centred(key_of[8], (INNER_DIM, MODEL_DIM), INNER_DIM ** -0.5, 0.09375, ((1, 8),))
    residual = centred(key_of[9], (STRING_LENGTH, MODEL_DIM), 1.0, 6.0, ((0, 32),))
    ffn_gain = jnp.clip(1.0 + 0.1 * jax.random.normal(key_of[10], (MODEL_DIM,), jnp.float32), 0.5, 1.5)
    router = centred(key_of[11], (MODEL_DIM, EXPERTS), MODEL_DIM ** -0.5, 0.125, (), jnp.float32)
    routes_keys = jax.random.split(jax.random.fold_in(key_of[12], 1), STRING_LENGTH // TOK_DEV)
    routes_turns = jax.random.permutation(jax.random.fold_in(key_of[12], 3), STRING_LENGTH // TOK_DEV)
    routes = jax.vmap(lambda own, number: routed_block(jax.random.fold_in(key_of[12], 2), own, number, TOK_DEV, EXPERTS, 2, SLOT_CAP, 2))(routes_keys, routes_turns).reshape((STRING_LENGTH, 2))
    gate_weight = centred(key_of[13], (EXPERTS, MODEL_DIM, HIDDEN_DIM), MODEL_DIM ** -0.5, 0.125, ((0, 4), (2, 8)))
    up_weight = centred(key_of[14], (EXPERTS, MODEL_DIM, HIDDEN_DIM), MODEL_DIM ** -0.5, 0.125, ((0, 4), (2, 8)))
    down_weight = centred(key_of[15], (EXPERTS, HIDDEN_DIM, MODEL_DIM), HIDDEN_DIM ** -0.5, 0.0625, ((0, 4), (1, 8)))
    return dict(ssm_input=ssm_input, gate_input=gate_input, step_size=step_size, decay_rate=decay_rate, in_coeff=in_coeff, out_coeff=out_coeff, skip_gain=skip_gain, norm_gain=norm_gain, out_proj=out_proj, residual=residual, ffn_gain=ffn_gain, router=router, routes=routes, gate_weight=gate_weight, up_weight=up_weight, down_weight=down_weight)


EPSILON = 1e-05
HIGHEST_PREC = lax.Precision.HIGHEST

def rms_scale(values, gain_vec):
    return values * lax.rsqrt(lax.optimization_barrier(jnp.mean(values * values, axis=-1, keepdims=True)) + EPSILON) * gain_vec

def slot_tables(routes_block, expert_count, slot_cap):
    blocks, row_total = (routes_block.shape[0], routes_block.shape[1])
    flat_routes = routes_block.reshape(blocks, row_total * 2)
    onehot = (flat_routes[:, :, None] == jnp.arange(expert_count, dtype=jnp.int32)[None, None, :]).astype(jnp.int32)
    earlier = jnp.cumsum(onehot, axis=1) - onehot
    slot_rank = lax.optimization_barrier(jnp.sum(earlier * onehot, axis=2))
    slot_index = (flat_routes * slot_cap + slot_rank).reshape(blocks, row_total, 2)
    placed = slot_index[:, :, :, None] == jnp.arange(expert_count * slot_cap, dtype=jnp.int32)[None, None, None, :]
    return placed.astype(jnp.float32)

def reference(ssm_input, gate_input, step_size, decay_rate, in_coeff, out_coeff, skip_gain, norm_gain, out_proj, residual, ffn_gain, router, routes, gate_weight, up_weight, down_weight):
    inputs_f = ssm_input.astype(jnp.float32).reshape(STRING_LENGTH, NUM_HEADS, HEAD_DIM)
    in_float = in_coeff.astype(jnp.float32)
    out_float = out_coeff.astype(jnp.float32)

    def advance(ssm_state, token_row):
        x_row, step_row, in_row, out_row = token_row
        factor = jnp.exp(-step_row * decay_rate)
        ssm_state = factor[:, None, None] * ssm_state + (step_row[:, None] * x_row)[:, :, None] * in_row[None, None, :]
        output = jnp.einsum('hpn,n->hp', ssm_state, out_row, precision=HIGHEST_PREC)
        return (ssm_state, output)
    initial = jnp.zeros((NUM_HEADS, HEAD_DIM, STATE_DIM), jnp.float32)
    final_state, scanned = lax.scan(advance, initial, (inputs_f, step_size, in_float, out_float))
    ssm_out = scanned + skip_gain[None, :, None] * inputs_f
    gated_out = ssm_out.reshape(STRING_LENGTH, INNER_DIM) * jax.nn.silu(gate_input.astype(jnp.float32))
    mixed_rows = rms_scale(gated_out, norm_gain).astype(jnp.bfloat16)
    mamba_out = jnp.dot(mixed_rows, out_proj, preferred_element_type=jnp.float32).astype(jnp.bfloat16)
    hidden_res = (residual.astype(jnp.float32) + mamba_out.astype(jnp.float32)).astype(jnp.bfloat16)
    hidden_float = hidden_res.astype(jnp.float32)
    normed = rms_scale(hidden_float, ffn_gain).astype(jnp.bfloat16)
    logits = jnp.dot(normed.astype(jnp.float32), router, precision=HIGHEST_PREC)
    expert_ids = jnp.arange(EXPERTS, dtype=jnp.int32)[None, :]
    first_logit = lax.optimization_barrier(jnp.sum(logits * (routes[:, 0:1] == expert_ids).astype(jnp.float32), axis=1))
    second_logit = lax.optimization_barrier(jnp.sum(logits * (routes[:, 1:2] == expert_ids).astype(jnp.float32), axis=1))
    first_prob = jax.nn.sigmoid(first_logit - second_logit)
    second_prob = 1.0 - first_prob
    blocks = STRING_LENGTH // TOK_DEV
    placed = slot_tables(routes.reshape(blocks, TOK_DEV, 2), EXPERTS, SLOT_CAP)
    filled = lax.optimization_barrier(jnp.sum(placed, axis=2))
    normed_blocks = normed.astype(jnp.float32).reshape(blocks, TOK_DEV, MODEL_DIM)
    dispatch = jnp.einsum('brs,brm->bsm', filled, normed_blocks, precision=HIGHEST_PREC).astype(jnp.bfloat16)
    dispatch = dispatch.reshape(blocks, EXPERTS, SLOT_CAP, MODEL_DIM).transpose(1, 0, 2, 3)
    block_count = HIDDEN_DIM // HID_DEV

    def run_expert(operands):
        expert_rows, gate_w, up_w, down_w = operands
        flat_rows = expert_rows.reshape(blocks * SLOT_CAP, MODEL_DIM)
        gate_act = jnp.dot(flat_rows, gate_w, preferred_element_type=jnp.float32)
        up_act = jnp.dot(flat_rows, up_w, preferred_element_type=jnp.float32)
        hidden = (jax.nn.silu(gate_act) * up_act).astype(jnp.bfloat16)
        hidden_blocks = hidden.reshape(blocks * SLOT_CAP, block_count, HID_DEV).transpose(1, 0, 2)
        down_blocks = down_w.reshape(block_count, HID_DEV, MODEL_DIM)

        def add_block(running, pair_in):
            partial_sum = jnp.dot(pair_in[0], pair_in[1], preferred_element_type=jnp.float32).astype(jnp.bfloat16)
            partial_sum = lax.optimization_barrier(partial_sum)
            return (running + partial_sum.astype(jnp.float32), None)
        summed, unused = lax.scan(add_block, jnp.zeros((blocks * SLOT_CAP, MODEL_DIM), jnp.float32), (hidden_blocks, down_blocks))
        return summed.astype(jnp.bfloat16).reshape(blocks, SLOT_CAP, MODEL_DIM)
    expert_out = lax.map(run_expert, (dispatch, gate_weight, up_weight, down_weight))
    returned = expert_out.transpose(1, 0, 2, 3).reshape(blocks, EXPERTS * SLOT_CAP, MODEL_DIM).astype(jnp.float32)
    first_blocks = first_prob.reshape(blocks, TOK_DEV)
    second_blocks = second_prob.reshape(blocks, TOK_DEV)
    weights = first_blocks[:, :, None] * placed[:, :, 0, :] + second_blocks[:, :, None] * placed[:, :, 1, :]
    contrib = jnp.einsum('brs,bsm->brm', weights, returned, precision=HIGHEST_PREC).reshape(STRING_LENGTH, MODEL_DIM)
    return (hidden_float + contrib).astype(jnp.bfloat16)
```

```python
import jax
import jax.numpy as jnp
from jax import lax
from jax.experimental import pallas as pl
from jax.experimental.pallas import tpu as pltpu
from jax.sharding import PartitionSpec as P

EPSILON = 1e-05
HIGHEST_PREC = lax.Precision.HIGHEST


def rms_scale(values, gain_vec):
    return (
        values * lax.rsqrt(jnp.mean(values * values, axis=-1, keepdims=True) + EPSILON) * gain_vec
    )


def slot_tables(routes_block, expert_count, slot_cap):
    blocks, row_total = (routes_block.shape[0], routes_block.shape[1])
    flat_routes = routes_block.reshape(blocks, row_total * 2)
    onehot = (
        flat_routes[:, :, None] == jnp.arange(expert_count, dtype=jnp.int32)[None, None, :]
    ).astype(jnp.int32)
    rank = jnp.arange(row_total * 2)
    before = (rank[:, None] > rank[None, :]).astype(jnp.int32)
    earlier = jnp.sum(before[None, :, :, None] * onehot[:, None, :, :], axis=2)
    slot_rank = jnp.sum(earlier * onehot, axis=2)
    slot_index = (flat_routes * slot_cap + slot_rank).reshape(blocks, row_total, 2)
    placed = (
        slot_index[:, :, :, None]
        == jnp.arange(expert_count * slot_cap, dtype=jnp.int32)[None, None, None, :]
    )
    return placed.astype(jnp.float32)


def shards(
    ssm_input,
    gate_input,
    step_size,
    decay_rate,
    in_coeff,
    out_coeff,
    skip_gain,
    norm_gain,
    out_proj,
    residual,
    ffn_gain,
    router,
    routes,
    gate_weight,
    up_weight,
    down_weight,
):
    tok_rows = ssm_input.shape[0]
    head_count = step_size.shape[1]
    head_width = ssm_input.shape[1] // head_count
    dev_count = lax.axis_size("dev")
    inner_dim = ssm_input.shape[1] * dev_count
    block_rows = residual.shape[0]
    model_dim = residual.shape[1]
    experts = lax.axis_size("grp")
    slot_cap = max(2, 4 * block_rows // experts)
    group_slots = experts * slot_cap
    inputs_f = ssm_input.astype(jnp.float32).reshape(tok_rows, head_count, head_width)
    in_float = in_coeff.astype(jnp.float32)
    out_float = out_coeff.astype(jnp.float32)
    log_rate = -(step_size * decay_rate[None, :])
    lower = jnp.arange(tok_rows)[:, None] >= jnp.arange(tok_rows)[None, :]
    cumulative = jnp.dot(lower.astype(jnp.float32), log_rate, precision=HIGHEST_PREC)
    causal = (jnp.arange(tok_rows)[:, None] >= jnp.arange(tok_rows)[None, :])[:, :, None]
    spread = cumulative[:, None, :] - cumulative[None, :, :]
    decay_pair = jnp.where(causal, jnp.exp(jnp.where(causal, spread, 0.0)), 0.0)
    scores = jnp.dot(out_coeff, in_coeff.T, preferred_element_type=jnp.float32)
    mixing = decay_pair * scores[:, :, None] * step_size[None, :, :]
    inside = jnp.einsum("tuh,uhp->thp", mixing, inputs_f, precision=HIGHEST_PREC)
    to_end = jnp.exp(cumulative[-1][None, :] - cumulative) * step_size
    own_state = jnp.einsum("uh,uhp,un->hpn", to_end, inputs_f, in_float, precision=HIGHEST_PREC)
    own_log = cumulative[-1]
    group_logs, group_states = (
        lax.all_gather(own_log[None].astype(jnp.bfloat16), "grp", axis=0, tiled=True).astype(
            jnp.float32
        ),
        lax.all_gather(own_state[None].astype(jnp.bfloat16), "grp", axis=0, tiled=True).astype(
            jnp.float32
        ),
    )
    group_index = jnp.arange(group_logs.shape[0])
    my_group = lax.axis_index("grp")
    inclusive = jnp.sum(
        jnp.where((group_index[:, None] >= group_index[None, :])[:, :, None], group_logs[None], 0.0),
        axis=1,
    )
    exclusive = inclusive - group_logs
    before_me = jnp.sum(jnp.where((group_index == my_group)[:, None], exclusive, 0.0), axis=0)
    earlier_mask = (group_index < my_group)[:, None]
    weighting = jnp.where(
        earlier_mask, jnp.exp(jnp.where(earlier_mask, before_me[None, :] - inclusive, 0.0)), 0.0
    )
    entering = jnp.einsum("gh,ghpn->hpn", weighting, group_states, precision=HIGHEST_PREC)
    carried = jnp.exp(cumulative)[:, :, None] * jnp.einsum(
        "hpn,tn->thp", entering, out_float, precision=HIGHEST_PREC
    )
    ssm_out = inside + carried + skip_gain[None, :, None] * inputs_f
    gated_out = ssm_out.reshape(tok_rows, head_count * head_width) * jax.nn.silu(
        gate_input.astype(jnp.float32)
    )
    squares = lax.psum(jnp.sum(gated_out * gated_out, axis=1), "dev")
    mixed_rows = (
        gated_out * lax.rsqrt(squares[:, None] / inner_dim + EPSILON) * norm_gain[None, :]
    ).astype(jnp.bfloat16)
    projected = jnp.dot(
        lax.all_gather(mixed_rows, "dev", axis=1, tiled=True),
        out_proj,
        preferred_element_type=jnp.float32,
    ).astype(jnp.bfloat16)
    mamba_out = lax.all_to_all(projected, "dev", split_axis=0, concat_axis=1, tiled=True)
    hidden_res = (residual.astype(jnp.float32) + mamba_out.astype(jnp.float32)).astype(jnp.bfloat16)
    hidden_float = hidden_res.astype(jnp.float32)
    normed = rms_scale(hidden_float, ffn_gain).astype(jnp.bfloat16)
    logits = jnp.dot(normed.astype(jnp.float32), router, precision=HIGHEST_PREC)
    expert_ids = jnp.arange(experts, dtype=jnp.int32)[None, :]
    first_logit = jnp.sum(logits * (routes[:, 0:1] == expert_ids).astype(jnp.float32), axis=1)
    second_logit = jnp.sum(logits * (routes[:, 1:2] == expert_ids).astype(jnp.float32), axis=1)
    first_prob = jax.nn.sigmoid(first_logit - second_logit)
    second_prob = 1.0 - first_prob
    placed = slot_tables(routes[None], experts, slot_cap)[0]
    filled = jnp.sum(placed, axis=1)
    outgoing = jnp.dot(
        filled.T.astype(jnp.bfloat16), normed, preferred_element_type=jnp.float32
    ).astype(jnp.bfloat16)
    outgoing = outgoing.reshape(experts, slot_cap, model_dim)
    arrived = lax.all_to_all(outgoing, "grp", split_axis=0, concat_axis=0, tiled=True)
    all_rows = lax.all_gather(arrived, "dev", axis=0, tiled=True).reshape(-1, model_dim)
    gate_act = jnp.dot(all_rows, gate_weight[0], preferred_element_type=jnp.float32)
    up_act = jnp.dot(all_rows, up_weight[0], preferred_element_type=jnp.float32)
    hidden = (jax.nn.silu(gate_act) * up_act).astype(jnp.bfloat16)
    summed = lax.psum_scatter(
        jnp.dot(hidden, down_weight[0], preferred_element_type=jnp.float32).astype(jnp.bfloat16),
        "dev",
        scatter_dimension=0,
        tiled=True,
    )
    returned = lax.all_to_all(
        summed.reshape(experts, slot_cap, model_dim), "grp", split_axis=0, concat_axis=0, tiled=True
    )
    weights = first_prob[:, None] * placed[:, 0, :] + second_prob[:, None] * placed[:, 1, :]
    contrib = jnp.dot(
        weights,
        returned.reshape(group_slots, model_dim).astype(jnp.float32),
        precision=HIGHEST_PREC,
    )
    return (hidden_float + contrib).astype(jnp.bfloat16)


ACROSS_X, ACROSS_Y, ACROSS_CORE = 1, 2, 4
GATHER_ORDER = (0, 4, 1, 2, 5, 6, 3, 7)
BF16, F32 = jnp.bfloat16, jnp.float32


def fused_kernel(
    ssm, gate, step, decay, in_c, out_c, skip, gain, res, ffn, router, routes,
    wp_hbm, wg_hbm, wu_hbm, wd_hbm,
    out,
    wp, wg, wu, wd, own_state, st_in, st_out, y_buf, g_all, ss_send, ss_recv, pr_send, pr_recv,
    hid, x_all, h_buf, part, core_in, acc, x_in, y_in, mid, y_in2, x_in2, fin, z_in,
    w_sem, st_s, st_r, ag_s, ag_r, ss_s, ss_r, pr_s, pr_r, zx_s, zx_r, rs_s, rs_r,
):
    z, d = lax.axis_index("grp"), lax.axis_index("dev")
    rows, chans = ssm.shape
    heads = step.shape[1]
    width = chans // heads
    n_state = in_c.shape[1]
    tok, dim = res.shape
    half = dim // 2
    hidden_units = wg.shape[1]
    cols = wp.shape[1]
    core0, x0, y0 = lax.rem(d, 2), lax.rem(lax.div(d, 2), 2), lax.div(d, 4)

    def dev_of(r):
        c = 1 - core0 if r & ACROSS_CORE else core0
        x = 1 - x0 if r & ACROSS_X else x0
        y = 1 - y0 if r & ACROSS_Y else y0
        return (y * 2 + x) * 2 + c

    def grp_of(k):
        return (z, z + 1 - 2 * lax.rem(z, 2), lax.rem(z + 2, 4), 3 - z)[k]

    sent = []

    def push(src, dst, s_sem, r_sem, to):
        copy = pltpu.make_async_remote_copy(
            src_ref=src, dst_ref=dst, send_sem=s_sem, recv_sem=r_sem,
            device_id=to, device_id_type=pl.DeviceIdType.MESH,
        )
        copy.start()
        sent.append(copy)

    def arrived(dst, s_sem, r_sem, to):
        pltpu.make_async_remote_copy(
            src_ref=dst, dst_ref=dst, send_sem=s_sem, recv_sem=r_sem,
            device_id=to, device_id_type=pl.DeviceIdType.MESH,
        ).wait_recv()

    loads = [
        pltpu.make_async_copy(wp_hbm, wp, w_sem.at[0]),
        pltpu.make_async_copy(wg_hbm.at[0], wg, w_sem.at[1]),
        pltpu.make_async_copy(wu_hbm.at[0], wu, w_sem.at[2]),
        pltpu.make_async_copy(wd_hbm.at[0], wd, w_sem.at[3]),
    ]
    for load in loads:
        load.start()

    barrier = pltpu.get_barrier_semaphore()
    for r in range(1, 8):
        pl.semaphore_signal(
            barrier, inc=1, device_id=(z, dev_of(r)), device_id_type=pl.DeviceIdType.MESH
        )
    for k in range(1, 4):
        pl.semaphore_signal(
            barrier, inc=1, device_id=(grp_of(k), d), device_id_type=pl.DeviceIdType.MESH
        )

    def iota(shape, axis):
        return lax.broadcasted_iota(jnp.int32, shape, axis)

    def exact(a, b):
        return jnp.dot(a, b, precision=HIGHEST_PREC, preferred_element_type=F32)

    causal = iota((rows, rows), 0) >= iota((rows, rows), 1)
    pad = (iota((heads, 128), 0) == iota((heads, 128), 1)).astype(F32)
    expand = (iota((128, chans), 0) == lax.div(iota((128, chans), 1), width)).astype(F32)
    log_pad = exact(-(step[...] * decay[...]), pad)
    step_pad = exact(step[...], pad)
    cum = exact(causal.astype(F32), log_pad)
    cum_t, step_t = cum.T, step_pad.T
    cum_wide, step_wide = exact(cum, expand), exact(step_pad, expand)
    last = cum_wide[rows - 1 : rows]
    xf = ssm[...].astype(F32)
    weighted = (jnp.exp(last - cum_wide) * step_wide * xf).astype(BF16)
    in_t = in_c[...].astype(F32).T.astype(BF16)
    own_state[...] = jnp.dot(in_t, weighted, preferred_element_type=F32)
    group_decay = jnp.exp(last)
    pl.semaphore_wait(barrier, 10)

    pieces = st_in.shape[0]
    pw = chans // pieces

    def state_copy(c):
        return pltpu.make_async_remote_copy(
            src_ref=st_out.at[c], dst_ref=st_in.at[c], send_sem=st_s.at[c], recv_sem=st_r.at[c],
            device_id=(lax.rem(z + 1, 4), d), device_id_type=pl.DeviceIdType.MESH,
        )

    def relay(c):
        at = slice(c * pw, (c + 1) * pw)
        state_copy(c).wait_recv()
        st_out[c] = (group_decay[:, at] * st_in[c].astype(F32) + own_state[:, at]).astype(BF16)
        state_copy(c).start()

    @pl.when(z == 0)
    def _():
        for c in range(pieces):
            st_out[c] = own_state[:, c * pw : (c + 1) * pw].astype(BF16)
            state_copy(c).start()
        st_in[...] = jnp.zeros_like(st_in)

    scores = lax.dot_general(
        out_c[...], in_c[...], (((1,), (1,)), ((), ())), preferred_element_type=F32
    )
    scores = jnp.where(causal, scores, 0.0)
    low_lane = iota((rows, 2 * width), 1) < width
    skip_wide = exact(jnp.broadcast_to(skip[...], (8, heads)), expand[0:heads])[0:1]

    def inside(c):
        at = slice(c * pw, (c + 1) * pw)
        x_pair = ssm[:, at]
        pair = []
        for h in (2 * c, 2 * c + 1):
            spread = cum[:, h : h + 1] - cum_t[h : h + 1, :]
            mixing = jnp.exp(jnp.minimum(spread, 0.0)) * scores * step_t[h : h + 1, :]
            pair.append(jnp.dot(mixing.astype(BF16), x_pair, preferred_element_type=F32))
        y_buf[:, at] = jnp.where(low_lane, pair[0], pair[1]) + skip_wide[:, at] * xf[:, at]

    def relay_at(group, first):
        @pl.when(z == group)
        def _():
            for c in (first, first + 1):
                relay(c)

    inside(0)
    relay_at(1, 0)
    inside(1)
    relay_at(1, 2)
    relay_at(2, 0)
    inside(2)
    relay_at(2, 2)
    inside(3)

    @pl.when(z == 3)
    def _():
        for c in range(pieces):
            state_copy(c).wait_recv()

    carried = jnp.concatenate(
        [jnp.dot(out_c[...], st_in[c], preferred_element_type=F32) for c in range(pieces)], axis=1
    )
    gf = gate[...].astype(F32)
    gated = (y_buf[...] + jnp.exp(cum_wide) * carried) * (gf / (1.0 + jnp.exp(-gf)))
    g_all[0] = (gated * gain[...]).astype(BF16)

    class Gather:
        def __init__(self, number, ref_at, length):
            self.n, self.at, self.length = number, ref_at, length

        def hop(self, src, through, lo, size, sem):
            dst = src ^ through
            push(
                self.at(src, lo, size), self.at(dst, lo, size),
                ag_s.at[self.n, sem], ag_r.at[self.n, sem], (z, dev_of(through)),
            )

        def wait(self, slot):
            if slot == 3:
                h = self.length // 2
                for lo, sem in ((0, 3), (h, 0)):
                    arrived(
                        self.at(3, lo, h), ag_s.at[self.n, sem], ag_r.at[self.n, sem], (z, d)
                    )
            else:
                arrived(
                    self.at(slot, 0, self.length),
                    ag_s.at[self.n, slot], ag_r.at[self.n, slot], (z, d),
                )

        def first(self):
            self.hop(0, ACROSS_X, 0, self.length, 1)
            self.hop(0, ACROSS_Y, 0, self.length, 2)
            self.hop(0, ACROSS_CORE, 0, self.length, 4)

        def second(self):
            h = self.length // 2
            self.wait(1)
            self.hop(1, ACROSS_Y, 0, h, 3)
            self.hop(1, ACROSS_CORE, 0, self.length, 5)
            self.wait(2)
            self.hop(2, ACROSS_X, h, h, 0)
            self.hop(2, ACROSS_CORE, 0, self.length, 6)

        def third(self):
            self.wait(3)
            self.hop(3, ACROSS_CORE, 0, self.length, 7)

        def rest(self):
            for slot in (4, 5, 6, 7):
                self.wait(slot)

    mixer = Gather(4, lambda r, lo, size: g_all.at[r, pl.ds(lo, size)], rows)
    mixer.first()
    squares = jnp.sum(gated * gated, axis=1, keepdims=True)
    ss_send[...] = jnp.broadcast_to(squares, ss_send.shape)

    def own_rows(r):
        return pl.ds(pl.multiple_of(dev_of(r) * tok, tok), tok)

    for r in range(1, 8):
        push(
            ss_send.at[own_rows(r)], ss_recv.at[d], ss_s.at[r], ss_r.at[r], (z, dev_of(r))
        )
    ss_recv[d] = ss_send[own_rows(0)]
    loads[0].wait()

    def project(r):
        w_rows = pl.ds(pl.multiple_of(dev_of(r) * chans, chans), chans)
        return jnp.dot(g_all[r], wp[w_rows, :], preferred_element_type=F32)

    total = project(0)
    mixer.second()
    mixer.wait(4)
    total = total + project(4)
    total = total + project(1)
    mixer.third()
    total = total + project(2)
    for r in (5, 6):
        mixer.wait(r)
        total = total + project(r)
    total = total + project(3)
    mixer.wait(7)
    total = total + project(7)
    pr_send[...] = total.astype(BF16)
    for r in range(1, 8):
        push(
            pr_send.at[own_rows(r)], pr_recv.at[d], pr_s.at[r], pr_r.at[r], (z, dev_of(r))
        )
    pr_recv[d] = pr_send[own_rows(0)]
    for r in range(1, 8):
        arrived(ss_recv.at[dev_of(r)], ss_s.at[r], ss_r.at[r], (z, d))
    norm = ss_recv[0]
    for j in range(1, 8):
        norm = norm + ss_recv[j]
    norm = lax.rsqrt(norm[:, 0:1] / (chans * 8) + EPSILON)
    for r in range(1, 8):
        arrived(pr_recv.at[dev_of(r)], pr_s.at[r], pr_r.at[r], (z, d))
    square = jnp.zeros((tok, cols), F32)
    for j in range(8):
        at = slice(j * cols, (j + 1) * cols)
        mamba = (pr_recv[j].astype(F32) * norm).astype(BF16).astype(F32)
        value = (res[:, at].astype(F32) + mamba).astype(BF16).astype(F32)
        hid[:, at] = value
        square = square + value * value
    inv = lax.rsqrt(jnp.sum(square, axis=1, keepdims=True) / dim + EPSILON)
    x_all[0, 0:tok] = (hid[...] * inv * ffn[...]).astype(BF16)

    for k in (1, 3, 2):
        push(
            x_all.at[0, 0:tok], x_all.at[k, 0:tok], zx_s.at[k], zx_r.at[k], (grp_of(k), d)
        )

    def chunk_view(k):
        return lambda r, lo, size: x_all.at[k, pl.ds(r * tok + lo, size)]

    gathers = [Gather(k, chunk_view(k), tok) for k in range(4)]
    turn = (0, 1, 3, 2)

    def gather_first(k):
        if k > 0:
            arrived(x_all.at[k, 0:tok], zx_s.at[k], zx_r.at[k], (z, d))
        gathers[k].first()

    gather_first(0)
    logits = exact(x_all[0, 0:tok].astype(F32), router[...])
    experts = logits.shape[1]
    ids = iota((tok, experts), 1)
    named0, named1 = routes[:, 0:1] == ids, routes[:, 1:2] == ids
    logit0 = jnp.sum(jnp.where(named0, logits, 0.0), axis=1, keepdims=True)
    logit1 = jnp.sum(jnp.where(named1, logits, 0.0), axis=1, keepdims=True)
    prob0 = 1.0 / (1.0 + jnp.exp(-(logit0 - logit1)))
    prob1 = 1.0 - prob0

    def expert_weight(e):
        return jnp.where(routes[:, 0:1] == e, prob0, 0.0) + jnp.where(
            routes[:, 1:2] == e, prob1, 0.0
        )

    gathers[0].second()
    gather_first(turn[1])
    gathers[0].third()
    for load in loads[1:]:
        load.wait()
    gathers[0].rest()
    tile = 256
    lower, upper = slice(0, half), slice(half, dim)
    core_rows = slice(4 * tok, 8 * tok)

    def gate_up(k, begin, end):
        @pl.loop(begin, end)
        def _(i):
            at = pl.ds(pl.multiple_of(i * tile, tile), tile)
            x = x_all[k]
            g = jnp.dot(x, wg[:, at], preferred_element_type=F32)
            u = jnp.dot(x, wu[:, at], preferred_element_type=F32)
            h_buf[:, at] = (g / (1.0 + jnp.exp(-g)) * u).astype(BF16)

    def down(k, begin, end):
        @pl.loop(begin, end)
        def _(i):
            at = pl.ds(pl.multiple_of(i * tile, tile), tile)
            part[k, :, at] = jnp.dot(
                h_buf[...], wd[:, at], preferred_element_type=F32
            ).astype(BF16)

    def rs_push(k, n, src, dst, through):
        push(src, dst, rs_s.at[k, n], rs_r.at[k, n], (z, dev_of(through)))

    def rs_wait(k, n, dst):
        arrived(dst, rs_s.at[k, n], rs_r.at[k, n], (z, d))

    def add(a, b):
        return (a.astype(F32) + b.astype(F32)).astype(BF16)

    def core_send(k, n):
        at = (lower, upper)[n]
        rs_push(k, n, part.at[k, core_rows, at], core_in.at[k, :, at], ACROSS_CORE)

    def reduce_first(k):
        rs_wait(k, 0, core_in.at[k, :, lower])
        acc[k, :, lower] = add(part[k, 0 : 4 * tok, lower], core_in[k, :, lower])
        rs_push(k, 2, acc.at[k, tok : 2 * tok, lower], x_in.at[k, 0:tok], ACROSS_X)
        rs_push(k, 3, acc.at[k, 3 * tok : 4 * tok, lower], x_in.at[k, tok : 2 * tok], ACROSS_X)
        rs_wait(k, 1, core_in.at[k, :, upper])
        acc[k, :, upper] = add(part[k, 0 : 4 * tok, upper], core_in[k, :, upper])
        rs_push(k, 4, acc.at[k, 2 * tok : 4 * tok, upper], y_in.at[k], ACROSS_Y)

    def reduce_second(k):
        rs_wait(k, 2, x_in.at[k, 0:tok])
        rs_wait(k, 3, x_in.at[k, tok : 2 * tok])
        mid[k, 0] = add(acc[k, 2 * tok : 3 * tok, lower], x_in[k, tok : 2 * tok])
        rs_push(k, 5, mid.at[k, 0], y_in2.at[k], ACROSS_Y)
        rs_wait(k, 4, y_in.at[k])
        mid[k, 1] = add(acc[k, tok : 2 * tok, upper], y_in[k, tok : 2 * tok])
        rs_push(k, 6, mid.at[k, 1], x_in2.at[k], ACROSS_X)

    def reduce_third(k):
        near_x = acc[k, 0:tok, lower].astype(F32) + x_in[k, 0:tok].astype(F32)
        near_y = acc[k, 0:tok, upper].astype(F32) + y_in[k, 0:tok].astype(F32)
        rs_wait(k, 5, y_in2.at[k])
        fin[k, :, lower] = add(near_x, y_in2[k])
        rs_wait(k, 6, x_in2.at[k])
        fin[k, :, upper] = add(near_y, x_in2[k])
        if k > 0:
            push(fin.at[k], z_in.at[k], rs_s.at[k, 7], rs_r.at[k, 7], (grp_of(k), d))

    gu, dn = hidden_units // tile, dim // tile
    for n in range(4):
        k = turn[n]
        before = turn[n - 1] if n > 0 else None
        after = turn[n + 1] if n < 3 else None
        if n > 0:
            gathers[k].rest()
        gate_up(k, 0, gu // 2)
        if after is not None:
            gathers[after].second()
        if n < 2:
            gather_first(turn[n + 2])
        if before is not None:
            reduce_first(before)
        gate_up(k, gu // 2, gu)
        if after is not None:
            gathers[after].third()
        if before is not None:
            reduce_second(before)
        down(k, 0, dn // 2)
        core_send(k, 0)
        if before is not None:
            reduce_third(before)
        down(k, dn // 2, dn)
        core_send(k, 1)
    reduce_first(turn[3])
    reduce_second(turn[3])
    reduce_third(turn[3])
    result = hid[...] + expert_weight(z) * fin[0].astype(F32)
    for k in (1, 3, 2):
        arrived(z_in.at[k], rs_s.at[k, 7], rs_r.at[k, 7], (z, d))
        result = result + expert_weight(grp_of(k)) * z_in[k].astype(F32)
    out[...] = result.astype(BF16)
    for copy in sent:
        copy.wait_send()

    @pl.when(z < 3)
    def _():
        for c in range(pieces):
            state_copy(c).wait_send()


def fused(
    ssm_input, gate_input, step_size, decay_rate, in_coeff, out_coeff, skip_gain, norm_gain,
    out_proj, residual, ffn_gain, router, routes, gate_weight, up_weight, down_weight,
):
    rows, chans = ssm_input.shape
    tok, dim = residual.shape
    units = gate_weight.shape[2]
    n_state = in_coeff.shape[1]
    cols = out_proj.shape[1]
    half = dim // 2
    in_vmem = pl.BlockSpec(memory_space=pltpu.VMEM)
    in_hbm = pl.BlockSpec(memory_space=pl.ANY)
    dma = pltpu.SemaphoreType.DMA
    return pl.pallas_call(
        fused_kernel,
        out_shape=jax.ShapeDtypeStruct((tok, dim), BF16),
        in_specs=[in_vmem] * 12 + [in_hbm] * 4,
        out_specs=in_vmem,
        scratch_shapes=[
            pltpu.VMEM(out_proj.shape, BF16),
            pltpu.VMEM((dim, units), BF16),
            pltpu.VMEM((dim, units), BF16),
            pltpu.VMEM((units, dim), BF16),
            pltpu.VMEM((n_state, chans), F32),
            pltpu.VMEM((4, n_state, chans // 4), BF16),
            pltpu.VMEM((4, n_state, chans // 4), BF16),
            pltpu.VMEM((rows, chans), F32),
            pltpu.VMEM((8, rows, chans), BF16),
            pltpu.VMEM((rows, 128), F32),
            pltpu.VMEM((8, tok, 128), F32),
            pltpu.VMEM((rows, cols), BF16),
            pltpu.VMEM((8, tok, cols), BF16),
            pltpu.VMEM((tok, dim), F32),
            pltpu.VMEM((4, 8 * tok, dim), BF16),
            pltpu.VMEM((8 * tok, units), BF16),
            pltpu.VMEM((4, 8 * tok, dim), BF16),
            pltpu.VMEM((4, 4 * tok, dim), BF16),
            pltpu.VMEM((4, 4 * tok, dim), BF16),
            pltpu.VMEM((4, 2 * tok, half), BF16),
            pltpu.VMEM((4, 2 * tok, half), BF16),
            pltpu.VMEM((4, 2, tok, half), BF16),
            pltpu.VMEM((4, tok, half), BF16),
            pltpu.VMEM((4, tok, half), BF16),
            pltpu.VMEM((4, tok, dim), BF16),
            pltpu.VMEM((4, tok, dim), BF16),
            dma((4,)),
            dma((4,)),
            dma((4,)),
            dma((5, 8)),
            dma((5, 8)),
            dma((8,)),
            dma((8,)),
            dma((8,)),
            dma((8,)),
            dma((4,)),
            dma((4,)),
            dma((4, 8)),
            dma((4, 8)),
        ],
        compiler_params=pltpu.CompilerParams(
            collective_id=0, has_side_effects=True, vmem_limit_bytes=56 * 1024 * 1024
        ),
    )(
        ssm_input, gate_input, step_size, decay_rate[None], in_coeff, out_coeff, skip_gain[None],
        norm_gain[None], residual, ffn_gain[None], router, routes,
        out_proj, gate_weight, up_weight, down_weight,
    )


def solution(mesh):
    placed = (
        P("grp", "dev"),
        P("grp", "dev"),
        P("grp", "dev"),
        P("dev"),
        P("grp", None),
        P("grp", None),
        P("dev"),
        P("dev"),
        P(None, "dev"),
        P(("grp", "dev"), None),
        P(),
        P(),
        P(("grp", "dev"), None),
        P("grp", None, "dev"),
        P("grp", None, "dev"),
        P("grp", "dev", None),
    )
    small = mesh.shape["grp"] == 4 and mesh.shape["dev"] == 8
    return jax.shard_map(
        fused if small else shards, mesh=mesh, in_specs=placed, out_specs=P(("grp", "dev"), None), check_vma=False
    )
```

```python
import jax
import jax.numpy as jnp
from jax import lax
from jax.experimental import pallas as pl
from jax.experimental.pallas import tpu as pltpu
from jax.sharding import PartitionSpec as P

EPSILON = 1e-05
HIGHEST_PREC = lax.Precision.HIGHEST


def rms_scale(values, gain_vec):
    return (
        values * lax.rsqrt(jnp.mean(values * values, axis=-1, keepdims=True) + EPSILON) * gain_vec
    )


def slot_tables(routes_block, expert_count, slot_cap):
    blocks, row_total = (routes_block.shape[0], routes_block.shape[1])
    flat_routes = routes_block.reshape(blocks, row_total * 2)
    onehot = (
        flat_routes[:, :, None] == jnp.arange(expert_count, dtype=jnp.int32)[None, None, :]
    ).astype(jnp.int32)
    rank = jnp.arange(row_total * 2)
    before = (rank[:, None] > rank[None, :]).astype(jnp.int32)
    earlier = jnp.sum(before[None, :, :, None] * onehot[:, None, :, :], axis=2)
    slot_rank = jnp.sum(earlier * onehot, axis=2)
    slot_index = (flat_routes * slot_cap + slot_rank).reshape(blocks, row_total, 2)
    placed = (
        slot_index[:, :, :, None]
        == jnp.arange(expert_count * slot_cap, dtype=jnp.int32)[None, None, None, :]
    )
    return placed.astype(jnp.float32)


def shards(
    ssm_input,
    gate_input,
    step_size,
    decay_rate,
    in_coeff,
    out_coeff,
    skip_gain,
    norm_gain,
    out_proj,
    residual,
    ffn_gain,
    router,
    routes,
    gate_weight,
    up_weight,
    down_weight,
):
    tok_rows = ssm_input.shape[0]
    head_count = step_size.shape[1]
    head_width = ssm_input.shape[1] // head_count
    dev_count = lax.axis_size("dev")
    inner_dim = ssm_input.shape[1] * dev_count
    block_rows = residual.shape[0]
    model_dim = residual.shape[1]
    experts = lax.axis_size("grp")
    slot_cap = max(2, 4 * block_rows // experts)
    group_slots = experts * slot_cap
    inputs_f = ssm_input.astype(jnp.float32).reshape(tok_rows, head_count, head_width)
    in_float = in_coeff.astype(jnp.float32)
    out_float = out_coeff.astype(jnp.float32)
    log_rate = -(step_size * decay_rate[None, :])
    lower = jnp.arange(tok_rows)[:, None] >= jnp.arange(tok_rows)[None, :]
    cumulative = jnp.dot(lower.astype(jnp.float32), log_rate, precision=HIGHEST_PREC)
    causal = (jnp.arange(tok_rows)[:, None] >= jnp.arange(tok_rows)[None, :])[:, :, None]
    spread = cumulative[:, None, :] - cumulative[None, :, :]
    decay_pair = jnp.where(causal, jnp.exp(jnp.where(causal, spread, 0.0)), 0.0)
    scores = jnp.dot(out_coeff, in_coeff.T, preferred_element_type=jnp.float32)
    mixing = decay_pair * scores[:, :, None] * step_size[None, :, :]
    inside = jnp.einsum("tuh,uhp->thp", mixing, inputs_f, precision=HIGHEST_PREC)
    to_end = jnp.exp(cumulative[-1][None, :] - cumulative) * step_size
    own_state = jnp.einsum("uh,uhp,un->hpn", to_end, inputs_f, in_float, precision=HIGHEST_PREC)
    own_log = cumulative[-1]
    group_logs, group_states = (
        lax.all_gather(own_log[None].astype(jnp.bfloat16), "grp", axis=0, tiled=True).astype(
            jnp.float32
        ),
        lax.all_gather(own_state[None].astype(jnp.bfloat16), "grp", axis=0, tiled=True).astype(
            jnp.float32
        ),
    )
    group_index = jnp.arange(group_logs.shape[0])
    my_group = lax.axis_index("grp")
    inclusive = jnp.sum(
        jnp.where((group_index[:, None] >= group_index[None, :])[:, :, None], group_logs[None], 0.0),
        axis=1,
    )
    exclusive = inclusive - group_logs
    before_me = jnp.sum(jnp.where((group_index == my_group)[:, None], exclusive, 0.0), axis=0)
    earlier_mask = (group_index < my_group)[:, None]
    weighting = jnp.where(
        earlier_mask, jnp.exp(jnp.where(earlier_mask, before_me[None, :] - inclusive, 0.0)), 0.0
    )
    entering = jnp.einsum("gh,ghpn->hpn", weighting, group_states, precision=HIGHEST_PREC)
    carried = jnp.exp(cumulative)[:, :, None] * jnp.einsum(
        "hpn,tn->thp", entering, out_float, precision=HIGHEST_PREC
    )
    ssm_out = inside + carried + skip_gain[None, :, None] * inputs_f
    gated_out = ssm_out.reshape(tok_rows, head_count * head_width) * jax.nn.silu(
        gate_input.astype(jnp.float32)
    )
    squares = lax.psum(jnp.sum(gated_out * gated_out, axis=1), "dev")
    mixed_rows = (
        gated_out * lax.rsqrt(squares[:, None] / inner_dim + EPSILON) * norm_gain[None, :]
    ).astype(jnp.bfloat16)
    projected = jnp.dot(
        lax.all_gather(mixed_rows, "dev", axis=1, tiled=True),
        out_proj,
        preferred_element_type=jnp.float32,
    ).astype(jnp.bfloat16)
    mamba_out = lax.all_to_all(projected, "dev", split_axis=0, concat_axis=1, tiled=True)
    hidden_res = (residual.astype(jnp.float32) + mamba_out.astype(jnp.float32)).astype(jnp.bfloat16)
    hidden_float = hidden_res.astype(jnp.float32)
    normed = rms_scale(hidden_float, ffn_gain).astype(jnp.bfloat16)
    logits = jnp.dot(normed.astype(jnp.float32), router, precision=HIGHEST_PREC)
    expert_ids = jnp.arange(experts, dtype=jnp.int32)[None, :]
    first_logit = jnp.sum(logits * (routes[:, 0:1] == expert_ids).astype(jnp.float32), axis=1)
    second_logit = jnp.sum(logits * (routes[:, 1:2] == expert_ids).astype(jnp.float32), axis=1)
    first_prob = jax.nn.sigmoid(first_logit - second_logit)
    second_prob = 1.0 - first_prob
    placed = slot_tables(routes[None], experts, slot_cap)[0]
    filled = jnp.sum(placed, axis=1)
    outgoing = jnp.dot(
        filled.T.astype(jnp.bfloat16), normed, preferred_element_type=jnp.float32
    ).astype(jnp.bfloat16)
    outgoing = outgoing.reshape(experts, slot_cap, model_dim)
    arrived = lax.all_to_all(outgoing, "grp", split_axis=0, concat_axis=0, tiled=True)
    all_rows = lax.all_gather(arrived, "dev", axis=0, tiled=True).reshape(-1, model_dim)
    gate_act = jnp.dot(all_rows, gate_weight[0], preferred_element_type=jnp.float32)
    up_act = jnp.dot(all_rows, up_weight[0], preferred_element_type=jnp.float32)
    hidden = (jax.nn.silu(gate_act) * up_act).astype(jnp.bfloat16)
    summed = lax.psum_scatter(
        jnp.dot(hidden, down_weight[0], preferred_element_type=jnp.float32).astype(jnp.bfloat16),
        "dev",
        scatter_dimension=0,
        tiled=True,
    )
    returned = lax.all_to_all(
        summed.reshape(experts, slot_cap, model_dim), "grp", split_axis=0, concat_axis=0, tiled=True
    )
    weights = first_prob[:, None] * placed[:, 0, :] + second_prob[:, None] * placed[:, 1, :]
    contrib = jnp.dot(
        weights,
        returned.reshape(group_slots, model_dim).astype(jnp.float32),
        precision=HIGHEST_PREC,
    )
    return (hidden_float + contrib).astype(jnp.bfloat16)


ACROSS_X, ACROSS_Y, ACROSS_CORE = 1, 2, 4
GATHER_ORDER = (0, 4, 1, 2, 5, 6, 3, 7)
BF16, F32 = jnp.bfloat16, jnp.float32


def fused_kernel(
    ssm, gate, step, decay, in_c, out_c, skip, gain, res, ffn, router, routes,
    wp_hbm, wg_hbm, wu_hbm, wd_hbm,
    out,
    wp, wg, wu, wd, own_state, st_in, st_out, y_buf, g_all, ss_send, ss_recv, pr_send, pr_recv,
    hid, x_all, h_buf, part, core_in, acc, x_in, y_in, mid, y_in2, x_in2, fin, z_in,
    w_sem, st_s, st_r, ag_s, ag_r, ss_s, ss_r, pr_s, pr_r, zx_s, zx_r, rs_s, rs_r,
):
    z, d = lax.axis_index("grp"), lax.axis_index("dev")
    rows, chans = ssm.shape
    heads = step.shape[0]
    width = chans // heads
    n_state = in_c.shape[1]
    tok, dim = res.shape
    half = dim // 2
    hidden_units = wg.shape[1]
    cols = wp.shape[1]
    core0, x0, y0 = lax.rem(d, 2), lax.rem(lax.div(d, 2), 2), lax.div(d, 4)

    def dev_of(r):
        c = 1 - core0 if r & ACROSS_CORE else core0
        x = 1 - x0 if r & ACROSS_X else x0
        y = 1 - y0 if r & ACROSS_Y else y0
        return (y * 2 + x) * 2 + c

    def grp_of(k):
        return (z, z + 1 - 2 * lax.rem(z, 2), lax.rem(z + 2, 4), 3 - z)[k]

    sent = []

    def push(src, dst, s_sem, r_sem, to):
        copy = pltpu.make_async_remote_copy(
            src_ref=src, dst_ref=dst, send_sem=s_sem, recv_sem=r_sem,
            device_id=to, device_id_type=pl.DeviceIdType.MESH,
        )
        copy.start()
        sent.append(copy)

    def arrived(dst, s_sem, r_sem, to):
        pltpu.make_async_remote_copy(
            src_ref=dst, dst_ref=dst, send_sem=s_sem, recv_sem=r_sem,
            device_id=to, device_id_type=pl.DeviceIdType.MESH,
        ).wait_recv()

    loads = [
        pltpu.make_async_copy(wp_hbm, wp, w_sem.at[0]),
        pltpu.make_async_copy(wg_hbm.at[0], wg, w_sem.at[1]),
        pltpu.make_async_copy(wu_hbm.at[0], wu, w_sem.at[2]),
        pltpu.make_async_copy(wd_hbm.at[0], wd, w_sem.at[3]),
    ]
    for load in loads:
        load.start()

    barrier = pltpu.get_barrier_semaphore()
    for r in range(1, 8):
        pl.semaphore_signal(
            barrier, inc=1, device_id=(z, dev_of(r)), device_id_type=pl.DeviceIdType.MESH
        )
    for k in range(1, 4):
        pl.semaphore_signal(
            barrier, inc=1, device_id=(grp_of(k), d), device_id_type=pl.DeviceIdType.MESH
        )

    def iota(shape, axis):
        return lax.broadcasted_iota(jnp.int32, shape, axis)

    def exact(a, b):
        return jnp.dot(a, b, precision=HIGHEST_PREC, preferred_element_type=F32)

    def exact_t(a, b):
        return lax.dot_general(
            a, b, (((1,), (1,)), ((), ())), precision=HIGHEST_PREC, preferred_element_type=F32
        )

    causal = iota((rows, rows), 0) >= iota((rows, rows), 1)
    pad = (iota((heads, 128), 0) == iota((heads, 128), 1)).astype(F32)
    expand = (iota((128, chans), 0) == lax.div(iota((128, chans), 1), width)).astype(F32)
    pad_t = (iota((128, heads), 0) == iota((128, heads), 1)).astype(F32)
    decay_pad = exact(jnp.broadcast_to(decay[...], (8, heads)), pad)[0:1]
    step_t = exact(pad_t, step[...])
    step_pad = step_t.T
    log_pad = -(step_pad * decay_pad)
    cum = exact(causal.astype(F32), log_pad)
    cum_t = cum.T
    cum_wide, step_wide = exact(cum, expand), exact(step_pad, expand)
    last = cum_wide[rows - 1 : rows]
    xf = ssm[...].astype(F32)
    weighted = (jnp.exp(last - cum_wide) * step_wide * xf).astype(BF16)
    in_t = in_c[...].astype(F32).T.astype(BF16)
    own_state[...] = jnp.dot(in_t, weighted, preferred_element_type=F32)
    group_decay = jnp.exp(last)
    pl.semaphore_wait(barrier, 10)

    pieces = st_in.shape[0]
    pw = chans // pieces

    def state_copy(c):
        return pltpu.make_async_remote_copy(
            src_ref=st_out.at[c], dst_ref=st_in.at[c], send_sem=st_s.at[c], recv_sem=st_r.at[c],
            device_id=(lax.rem(z + 1, 4), d), device_id_type=pl.DeviceIdType.MESH,
        )

    def relay(c):
        at = slice(c * pw, (c + 1) * pw)
        state_copy(c).wait_recv()
        st_out[c] = (group_decay[:, at] * st_in[c].astype(F32) + own_state[:, at]).astype(BF16)
        state_copy(c).start()

    @pl.when(z == 0)
    def _():
        for c in range(pieces):
            st_out[c] = own_state[:, c * pw : (c + 1) * pw].astype(BF16)
            state_copy(c).start()
        st_in[...] = jnp.zeros_like(st_in)

    scores = lax.dot_general(
        out_c[...], in_c[...], (((1,), (1,)), ((), ())), preferred_element_type=F32
    )
    scores = jnp.where(causal, scores, 0.0)
    low_lane = iota((rows, 2 * width), 1) < width
    skip_wide = exact(jnp.broadcast_to(skip[...], (8, heads)), expand[0:heads])[0:1]

    def inside(c):
        at = slice(c * pw, (c + 1) * pw)
        x_pair = ssm[:, at]
        pair = []
        for h in (2 * c, 2 * c + 1):
            spread = cum[:, h : h + 1] - cum_t[h : h + 1, :]
            mixing = jnp.exp(jnp.minimum(spread, 0.0)) * scores * step_t[h : h + 1, :]
            pair.append(jnp.dot(mixing.astype(BF16), x_pair, preferred_element_type=F32))
        y_buf[:, at] = jnp.where(low_lane, pair[0], pair[1]) + skip_wide[:, at] * xf[:, at]

    def relay_at(group, first):
        @pl.when(z == group)
        def _():
            for c in (first, first + 1):
                relay(c)

    inside(0)
    relay_at(1, 0)
    inside(1)
    relay_at(1, 2)
    relay_at(2, 0)
    inside(2)
    relay_at(2, 2)
    inside(3)

    @pl.when(z == 3)
    def _():
        for c in range(pieces):
            state_copy(c).wait_recv()

    carried = jnp.concatenate(
        [jnp.dot(out_c[...], st_in[c], preferred_element_type=F32) for c in range(pieces)], axis=1
    )
    gf = gate[...].astype(F32)
    gated = (y_buf[...] + jnp.exp(cum_wide) * carried) * (gf / (1.0 + jnp.exp(-gf)))
    g_all[0] = (gated * gain[...]).astype(BF16)

    class Gather:
        def __init__(self, number, ref_at, length):
            self.n, self.at, self.length = number, ref_at, length

        def hop(self, src, through, lo, size, sem):
            dst = src ^ through
            push(
                self.at(src, lo, size), self.at(dst, lo, size),
                ag_s.at[self.n, sem], ag_r.at[self.n, sem], (z, dev_of(through)),
            )

        def wait(self, slot):
            if slot == 3:
                h = self.length // 2
                for lo, sem in ((0, 3), (h, 0)):
                    arrived(
                        self.at(3, lo, h), ag_s.at[self.n, sem], ag_r.at[self.n, sem], (z, d)
                    )
            else:
                arrived(
                    self.at(slot, 0, self.length),
                    ag_s.at[self.n, slot], ag_r.at[self.n, slot], (z, d),
                )

        def first(self):
            self.hop(0, ACROSS_X, 0, self.length, 1)
            self.hop(0, ACROSS_Y, 0, self.length, 2)
            self.hop(0, ACROSS_CORE, 0, self.length, 4)

        def second(self):
            h = self.length // 2
            self.wait(1)
            self.hop(1, ACROSS_Y, 0, h, 3)
            self.hop(1, ACROSS_CORE, 0, self.length, 5)
            self.wait(2)
            self.hop(2, ACROSS_X, h, h, 0)
            self.hop(2, ACROSS_CORE, 0, self.length, 6)

        def third(self):
            self.wait(3)
            self.hop(3, ACROSS_CORE, 0, self.length, 7)

        def rest(self):
            for slot in (4, 5, 6, 7):
                self.wait(slot)

    mixer = Gather(4, lambda r, lo, size: g_all.at[r, pl.ds(lo, size)], rows)
    mixer.first()
    squares = jnp.sum(gated * gated, axis=1, keepdims=True)
    ss_send[...] = jnp.broadcast_to(squares, ss_send.shape)

    def own_rows(r):
        return pl.ds(pl.multiple_of(dev_of(r) * tok, tok), tok)

    for r in range(1, 8):
        push(
            ss_send.at[own_rows(r)], ss_recv.at[d], ss_s.at[r], ss_r.at[r], (z, dev_of(r))
        )
    ss_recv[d] = ss_send[own_rows(0)]
    loads[0].wait()

    def project(r):
        w_rows = pl.ds(pl.multiple_of(dev_of(r) * chans, chans), chans)
        return jnp.dot(g_all[r], wp[w_rows, :], preferred_element_type=F32)

    total = project(0)
    mixer.second()
    mixer.wait(4)
    total = total + project(4)
    total = total + project(1)
    mixer.third()
    total = total + project(2)
    for r in (5, 6):
        mixer.wait(r)
        total = total + project(r)
    total = total + project(3)
    mixer.wait(7)
    total = total + project(7)
    pr_send[...] = total.astype(BF16)
    for r in range(1, 8):
        push(
            pr_send.at[own_rows(r)], pr_recv.at[d], pr_s.at[r], pr_r.at[r], (z, dev_of(r))
        )
    pr_recv[d] = pr_send[own_rows(0)]
    for r in range(1, 8):
        arrived(ss_recv.at[dev_of(r)], ss_s.at[r], ss_r.at[r], (z, d))
    norm = ss_recv[0]
    for j in range(1, 8):
        norm = norm + ss_recv[j]
    norm = lax.rsqrt(norm[:, 0:1] / (chans * 8) + EPSILON)
    for r in range(1, 8):
        arrived(pr_recv.at[dev_of(r)], pr_s.at[r], pr_r.at[r], (z, d))
    square = jnp.zeros((tok, cols), F32)
    for j in range(8):
        at = slice(j * cols, (j + 1) * cols)
        mamba = (pr_recv[j].astype(F32) * norm).astype(BF16).astype(F32)
        value = (res[:, at].astype(F32) + mamba).astype(BF16).astype(F32)
        hid[:, at] = value
        square = square + value * value
    inv = lax.rsqrt(jnp.sum(square, axis=1, keepdims=True) / dim + EPSILON)
    x_all[0, 0:tok] = (hid[...] * inv * ffn[...]).astype(BF16)

    for k in (1, 3, 2):
        push(
            x_all.at[0, 0:tok], x_all.at[k, 0:tok], zx_s.at[k], zx_r.at[k], (grp_of(k), d)
        )

    def chunk_view(k):
        return lambda r, lo, size: x_all.at[k, pl.ds(r * tok + lo, size)]

    gathers = [Gather(k, chunk_view(k), tok) for k in range(4)]
    turn = (0, 1, 3, 2)

    def gather_first(k):
        if k > 0:
            arrived(x_all.at[k, 0:tok], zx_s.at[k], zx_r.at[k], (z, d))
        gathers[k].first()

    gather_first(0)
    logits = exact_t(x_all[0, 0:tok].astype(F32), router[...])
    same = (iota((tok, tok), 0) == iota((tok, tok), 1)).astype(F32)
    named = exact_t(same, routes[...].astype(F32))
    experts = logits.shape[1]
    ids = iota((tok, experts), 1).astype(F32)
    named0, named1 = jnp.abs(named[:, 0:1] - ids) < 0.5, jnp.abs(named[:, 1:2] - ids) < 0.5
    logit0 = jnp.sum(jnp.where(named0, logits, 0.0), axis=1, keepdims=True)
    logit1 = jnp.sum(jnp.where(named1, logits, 0.0), axis=1, keepdims=True)
    prob0 = 1.0 / (1.0 + jnp.exp(-(logit0 - logit1)))
    prob1 = 1.0 - prob0

    def expert_weight(e):
        e = jnp.full((tok, 1), e, jnp.int32).astype(F32)
        return jnp.where(jnp.abs(named[:, 0:1] - e) < 0.5, prob0, 0.0) + jnp.where(
            jnp.abs(named[:, 1:2] - e) < 0.5, prob1, 0.0
        )

    gathers[0].second()
    gather_first(turn[1])
    gathers[0].third()
    for load in loads[1:]:
        load.wait()
    gathers[0].rest()
    tile = 256
    lower, upper = slice(0, half), slice(half, dim)
    core_rows = slice(4 * tok, 8 * tok)

    def gate_up(k, begin, end):
        @pl.loop(begin, end)
        def _(i):
            at = pl.ds(pl.multiple_of(i * tile, tile), tile)
            x = x_all[k]
            g = jnp.dot(x, wg[:, at], preferred_element_type=F32)
            u = jnp.dot(x, wu[:, at], preferred_element_type=F32)
            h_buf[:, at] = (g / (1.0 + jnp.exp(-g)) * u).astype(BF16)

    def down(k, begin, end):
        @pl.loop(begin, end)
        def _(i):
            at = pl.ds(pl.multiple_of(i * tile, tile), tile)
            part[k, :, at] = jnp.dot(
                h_buf[...], wd[:, at], preferred_element_type=F32
            ).astype(BF16)

    def rs_push(k, n, src, dst, through):
        push(src, dst, rs_s.at[k, n], rs_r.at[k, n], (z, dev_of(through)))

    def rs_wait(k, n, dst):
        arrived(dst, rs_s.at[k, n], rs_r.at[k, n], (z, d))

    def add(a, b):
        return (a.astype(F32) + b.astype(F32)).astype(BF16)

    def core_send(k, n):
        at = (lower, upper)[n]
        rs_push(k, n, part.at[k, core_rows, at], core_in.at[k, :, at], ACROSS_CORE)

    def reduce_first(k):
        rs_wait(k, 0, core_in.at[k, :, lower])
        acc[k, :, lower] = add(part[k, 0 : 4 * tok, lower], core_in[k, :, lower])
        rs_push(k, 2, acc.at[k, tok : 2 * tok, lower], x_in.at[k, 0:tok], ACROSS_X)
        rs_push(k, 3, acc.at[k, 3 * tok : 4 * tok, lower], x_in.at[k, tok : 2 * tok], ACROSS_X)
        rs_wait(k, 1, core_in.at[k, :, upper])
        acc[k, :, upper] = add(part[k, 0 : 4 * tok, upper], core_in[k, :, upper])
        rs_push(k, 4, acc.at[k, 2 * tok : 4 * tok, upper], y_in.at[k], ACROSS_Y)

    def reduce_second(k):
        rs_wait(k, 2, x_in.at[k, 0:tok])
        rs_wait(k, 3, x_in.at[k, tok : 2 * tok])
        mid[k, 0] = add(acc[k, 2 * tok : 3 * tok, lower], x_in[k, tok : 2 * tok])
        rs_push(k, 5, mid.at[k, 0], y_in2.at[k], ACROSS_Y)
        rs_wait(k, 4, y_in.at[k])
        mid[k, 1] = add(acc[k, tok : 2 * tok, upper], y_in[k, tok : 2 * tok])
        rs_push(k, 6, mid.at[k, 1], x_in2.at[k], ACROSS_X)

    def reduce_third(k):
        near_x = acc[k, 0:tok, lower].astype(F32) + x_in[k, 0:tok].astype(F32)
        near_y = acc[k, 0:tok, upper].astype(F32) + y_in[k, 0:tok].astype(F32)
        rs_wait(k, 5, y_in2.at[k])
        fin[k, :, lower] = add(near_x, y_in2[k])
        rs_wait(k, 6, x_in2.at[k])
        fin[k, :, upper] = add(near_y, x_in2[k])
        if k > 0:
            push(fin.at[k], z_in.at[k], rs_s.at[k, 7], rs_r.at[k, 7], (grp_of(k), d))

    gu, dn = hidden_units // tile, dim // tile
    for n in range(4):
        k = turn[n]
        before = turn[n - 1] if n > 0 else None
        after = turn[n + 1] if n < 3 else None
        if n > 0:
            gathers[k].rest()
        gate_up(k, 0, gu // 2)
        if after is not None:
            gathers[after].second()
        if n < 2:
            gather_first(turn[n + 2])
        if n > 1:
            reduce_third(turn[n - 2])
        if before is not None:
            reduce_first(before)
        gate_up(k, gu // 2, gu)
        if after is not None:
            gathers[after].third()
        down(k, 0, dn // 2)
        core_send(k, 0)
        if before is not None:
            reduce_second(before)
        down(k, dn // 2, dn)
        core_send(k, 1)
    reduce_first(turn[3])
    reduce_third(turn[2])
    reduce_second(turn[3])
    reduce_third(turn[3])
    result = hid[...] + expert_weight(z) * fin[0].astype(F32)
    for k in (1, 3, 2):
        arrived(z_in.at[k], rs_s.at[k, 7], rs_r.at[k, 7], (z, d))
        result = result + expert_weight(grp_of(k)) * z_in[k].astype(F32)
    out[...] = result.astype(BF16)
    for copy in sent:
        copy.wait_send()

    @pl.when(z < 3)
    def _():
        for c in range(pieces):
            state_copy(c).wait_send()


def fused(
    ssm_input, gate_input, step_size, decay_rate, in_coeff, out_coeff, skip_gain, norm_gain,
    out_proj, residual, ffn_gain, router, routes, gate_weight, up_weight, down_weight,
):
    rows, chans = ssm_input.shape
    tok, dim = residual.shape
    units = gate_weight.shape[2]
    n_state = in_coeff.shape[1]
    cols = out_proj.shape[1]
    half = dim // 2
    in_vmem = pl.BlockSpec(memory_space=pltpu.VMEM)
    in_hbm = pl.BlockSpec(memory_space=pl.ANY)
    dma = pltpu.SemaphoreType.DMA
    return pl.pallas_call(
        fused_kernel,
        out_shape=jax.ShapeDtypeStruct((tok, dim), BF16),
        in_specs=[in_vmem] * 12 + [in_hbm] * 4,
        out_specs=in_vmem,
        scratch_shapes=[
            pltpu.VMEM(out_proj.shape, BF16),
            pltpu.VMEM((dim, units), BF16),
            pltpu.VMEM((dim, units), BF16),
            pltpu.VMEM((units, dim), BF16),
            pltpu.VMEM((n_state, chans), F32),
            pltpu.VMEM((4, n_state, chans // 4), BF16),
            pltpu.VMEM((4, n_state, chans // 4), BF16),
            pltpu.VMEM((rows, chans), F32),
            pltpu.VMEM((8, rows, chans), BF16),
            pltpu.VMEM((rows, 128), F32),
            pltpu.VMEM((8, tok, 128), F32),
            pltpu.VMEM((rows, cols), BF16),
            pltpu.VMEM((8, tok, cols), BF16),
            pltpu.VMEM((tok, dim), F32),
            pltpu.VMEM((4, 8 * tok, dim), BF16),
            pltpu.VMEM((8 * tok, units), BF16),
            pltpu.VMEM((4, 8 * tok, dim), BF16),
            pltpu.VMEM((4, 4 * tok, dim), BF16),
            pltpu.VMEM((4, 4 * tok, dim), BF16),
            pltpu.VMEM((4, 2 * tok, half), BF16),
            pltpu.VMEM((4, 2 * tok, half), BF16),
            pltpu.VMEM((4, 2, tok, half), BF16),
            pltpu.VMEM((4, tok, half), BF16),
            pltpu.VMEM((4, tok, half), BF16),
            pltpu.VMEM((4, tok, dim), BF16),
            pltpu.VMEM((4, tok, dim), BF16),
            dma((4,)),
            dma((4,)),
            dma((4,)),
            dma((5, 8)),
            dma((5, 8)),
            dma((8,)),
            dma((8,)),
            dma((8,)),
            dma((8,)),
            dma((4,)),
            dma((4,)),
            dma((4, 8)),
            dma((4, 8)),
        ],
        compiler_params=pltpu.CompilerParams(
            collective_id=0, has_side_effects=True, vmem_limit_bytes=56 * 1024 * 1024
        ),
    )(
        ssm_input, gate_input, step_size.T, decay_rate[None], in_coeff, out_coeff, skip_gain[None],
        norm_gain[None], residual, ffn_gain[None], router.T, routes.T,
        out_proj, gate_weight, up_weight, down_weight,
    )


def solution(mesh):
    placed = (
        P("grp", "dev"),
        P("grp", "dev"),
        P("grp", "dev"),
        P("dev"),
        P("grp", None),
        P("grp", None),
        P("dev"),
        P("dev"),
        P(None, "dev"),
        P(("grp", "dev"), None),
        P(),
        P(),
        P(("grp", "dev"), None),
        P("grp", None, "dev"),
        P("grp", None, "dev"),
        P("grp", "dev", None),
    )
    small = mesh.shape["grp"] == 4 and mesh.shape["dev"] == 8
    return jax.shard_map(
        fused if small else shards, mesh=mesh, in_specs=placed, out_specs=P(("grp", "dev"), None), check_vma=False
    )
```
